256 devices in a mesh: blk: 64 (over y, x_lo, z), row: 4 (over x_hi, core).
Axes of the slice: x: 4 (x_hi: 2, x_lo: 2; x = x_hi * 2 + x_lo), y: 4, z: 8, core: 2. Of those that a mesh axis runs over, the one named last changes fastest.
Arguments:
- matrix: bfloat16 [49152, 16384], P(('row', 'blk'))
- pairing: int32 [2, 64, 4], replicated, may hold values from 0 to 3, each once within a row
Outputs:
- rotated_matrix: bfloat16 [49152, 16384], P(('row', 'blk'))
The draws below stay inside these ranges and needn't reach their ends.
Inputs may be any that keep to these rules, and one draw needn't show every extreme that they name: pairing[t, g] names each of the 4 slots once.
All inputs are finite; a program needn't handle non-finite values.
Results may differ from the reference program's by a relative error of at most 0.0062.
Values may be sent and summed in bfloat16 or wider, within the bound.
A program may use at most 128 MiB of HBM per device.

```python
import math
import jax
import jax.numpy as jnp
from jax import lax

BW = 64
BLK_DEV = 4
STEPS = 2
ROWS = 49152
COLS = 16384
N_BLK = 64


def draw_matrix(key, part):
    base_key = jax.random.fold_in(key, 11)
    keys = jax.random.split(base_key, 6)
    base = jax.random.normal(keys[0], (ROWS, COLS), jnp.float32)
    shared = jax.random.normal(keys[1], (ROWS, BW), jnp.float32)
    picks = jax.random.randint(keys[4], (8, COLS), 0, 4)
    loads = jax.random.normal(keys[5], (8, COLS), jnp.float32)
    common = jnp.zeros((ROWS, COLS), jnp.float32)
    for term_index in range(8):
        common = common + jnp.take(shared, picks[term_index], axis=1) * loads[term_index][None, :]
    common = common / math.sqrt(8.0)
    position = jnp.arange(ROWS, dtype=jnp.float32) / ROWS
    strength = jnp.exp(position * math.log(4.0))[:, None]
    col_gain = jnp.exp(jax.random.uniform(keys[2], (1, COLS), jnp.float32, math.log(0.3), math.log(3.0)))
    mixed = (base + strength * common) / jnp.sqrt(1.0 + strength * strength)
    return (mixed * col_gain).astype(jnp.bfloat16)


def setup_inputs(seed: int = 0) -> dict:
    arg_keys = jax.random.split(jax.random.key(seed), 3)
    matrix = draw_matrix(jax.random.fold_in(arg_keys[2], 71), 0)
    pairing = jax.vmap(lambda own: jax.random.permutation(own, BLK_DEV))(jax.random.split(arg_keys[1], STEPS * N_BLK)).reshape((STEPS, N_BLK, BLK_DEV)).astype(jnp.int32)
    return {"matrix": matrix, "pairing": pairing}


precise = lax.Precision.HIGHEST

def pair_rotation(cross_raw, squares):
    block_width = cross_raw.shape[0]
    col_scale = 1.0 / jnp.sqrt(squares + 1e-06)
    cross = 0.5 * cross_raw * col_scale[:block_width, None] * col_scale[None, block_width:]
    identity = jnp.eye(block_width, dtype=jnp.float32)
    left_factor = jnp.linalg.cholesky(identity + jnp.dot(cross, cross.T, precision=precise))
    right_factor = jnp.linalg.cholesky(identity + jnp.dot(cross.T, cross, precision=precise))
    left_inverse = jax.scipy.linalg.solve_triangular(left_factor, identity, lower=True).T
    right_inverse = jax.scipy.linalg.solve_triangular(right_factor, identity, lower=True).T
    upper_half = jnp.concatenate([left_inverse, jnp.dot(cross, right_inverse, precision=precise)], axis=1)
    lower_half = jnp.concatenate([-jnp.dot(cross.T, left_inverse, precision=precise), right_inverse], axis=1)
    return jnp.concatenate([upper_half, lower_half], axis=0).astype(jnp.bfloat16)

def rotate_couple(couple):
    gram = jnp.dot(couple.T.astype(jnp.float32), couple.astype(jnp.float32), preferred_element_type=jnp.float32)
    rotation = pair_rotation(gram[:BW, BW:], jnp.diagonal(gram))
    return jnp.dot(couple.astype(jnp.float32), rotation.astype(jnp.float32), preferred_element_type=jnp.float32).astype(jnp.bfloat16)

def reference(matrix, pairing):
    row_count = matrix.shape[0]
    current = matrix.reshape(row_count, N_BLK, BLK_DEV, BW)
    for turn_index in range(STEPS):
        current = jnp.take_along_axis(current, pairing[turn_index][None, :, :, None], axis=2)
        couples = jnp.moveaxis(current.reshape(row_count, N_BLK * (BLK_DEV // 2), 2 * BW), 1, 0)
        rotated = lax.map(rotate_couple, couples)
        current = jnp.moveaxis(rotated, 0, 1).reshape(row_count, N_BLK, BLK_DEV, BW)
        travelers = jnp.roll(current[:, :, 1::2], 1, axis=1)
        current = current.at[:, :, 1::2].set(travelers)
    return current.reshape(row_count, N_BLK * BLK_DEV * BW)
```

```python
import functools
import jax
import jax.numpy as jnp
from jax import lax
from jax.experimental import pallas as pl
from jax.experimental.pallas import tpu as pltpu
from jax.sharding import PartitionSpec as P

BW = 64
STEPS = 2
XH, XL, NY, NZ = 2, 2, 4, 8
NX = XH * XL
CHUNKS = NX * NY
PER = NZ // 2
GROUPS = CHUNKS * PER
COUPLES = 2 * GROUPS
ROWS_LOC = 192
CROSS_ROWS = 16 * NZ
PAY = CROSS_ROWS + 16
WIDE = 256 * PER
MESH = pl.DeviceIdType.MESH
HIGH = lax.Precision.HIGHEST


def lanes(shape):
    return lax.broadcasted_iota(jnp.int32, shape, len(shape) - 1)


def group_gram(pair, base, xg, j, gscr, pay_ref, squares):
    gscr[...] = lax.dot_general(
        xg, xg, (((0,), (0,)), ((), ())), preferred_element_type=jnp.float32
    )
    eye = (
        lax.broadcasted_iota(jnp.int32, (128, 128), 0)
        == lax.broadcasted_iota(jnp.int32, (128, 128), 1)
    )
    sq = [
        jnp.sum(jnp.where(eye, gscr[128 * t : 128 * t + 128, 128 * t : 128 * t + 128], 0.0),
                axis=0, keepdims=True)
        for t in range(2)
    ]
    lane16 = lanes((16, 128)) < BW
    lane1 = lanes((1, 128)) < BW
    row16 = lax.broadcasted_iota(jnp.int32, (16, 128), 0)
    for c in range(2):
        a = pair[base + 2 * c]
        b = pair[base + 2 * c + 1]
        rows = gscr[pl.ds(pl.multiple_of(a * BW, BW), BW), :]
        tile = jnp.where(b >= 2, rows[:, 128:], rows[:, :128])
        turned = pltpu.roll(tile, BW, 1)
        odd = (b % 2) == 1
        low = jnp.where(odd, turned, tile)
        high = jnp.where(odd, tile, turned)
        n = 2 * j + c
        for h in range(2):
            pay_ref[h, 0, 16 * n : 16 * n + 16, :] = jnp.where(
                lane16, low[32 * h : 32 * h + 16], high[32 * h + 16 : 32 * h + 32]
            ).astype(jnp.bfloat16)
        sa = jnp.where(a >= 2, sq[1], sq[0])
        sa = jnp.where((a % 2) == 1, pltpu.roll(sa, BW, 1), sa)
        sb = jnp.where(b >= 2, sq[1], sq[0])
        sb = jnp.where(odd, sb, pltpu.roll(sb, BW, 1))
        squares = jnp.where(row16 == n, jnp.where(lane1, sa, sb), squares)
    return squares


def put_squares(squares, pay_ref):
    for h in range(2):
        pay_ref[h, 0, CROSS_ROWS:, :] = squares.astype(jnp.bfloat16)


def gram_body(pair, x_ref, pay_ref, gscr):
    i = pl.program_id(0)
    squares = jnp.zeros((16, 128), jnp.float32)
    for j in range(PER):
        squares = group_gram(
            pair, (i * PER + j) * 4, x_ref[:, 256 * j : 256 * j + 256], j, gscr, pay_ref, squares
        )
    put_squares(squares, pay_ref)


def gram_call(pair, x):
    return pl.pallas_call(
        gram_body,
        out_shape=jax.ShapeDtypeStruct((2, CHUNKS, PAY, 128), jnp.bfloat16),
        grid_spec=pltpu.PrefetchScalarGridSpec(
            num_scalar_prefetch=1,
            grid=(CHUNKS,),
            in_specs=[pl.BlockSpec((ROWS_LOC, WIDE), lambda i, p: (0, i))],
            out_specs=pl.BlockSpec((2, 1, PAY, 128), lambda i, p: (0, i, 0, 0)),
            scratch_shapes=[pltpu.VMEM((256, 256), jnp.float32)],
        ),
    )(pair, x)


def rotate_group(pair, base, xg, left, right, wscr):
    lane = lanes((BW, 128)) < BW
    zero = jnp.zeros((BW, 128), jnp.bfloat16)
    for c in range(2):
        a = pair[base + 2 * c]
        b = pair[base + 2 * c + 1]
        top = jnp.where(lane, left[c], right[c])
        bot = pltpu.roll(jnp.where(lane, right[c], left[c]), BW, 1)
        for s in range(4):
            wscr[BW * s : BW * s + BW, 128 * c : 128 * c + 128] = jnp.where(
                a == s, top, jnp.where(b == s, bot, zero)
            )
    return jnp.dot(xg, wscr[...], preferred_element_type=jnp.float32).astype(jnp.bfloat16)


def apply_body(with_gram, pair, pair_next, x_ref, rot_ref, xlast_ref, rotlast_ref, *rest):
    if with_gram:
        out_ref, pay_ref, wscr, carry, gscr = rest
    else:
        out_ref, wscr, carry = rest
    i = pl.program_id(0)

    @pl.when(i == 0)
    def _():
        carry[...] = rotate_group(
            pair, (GROUPS - 1) * 4, xlast_ref[...],
            [rotlast_ref[0, c] for c in range(2)], [rotlast_ref[1, c] for c in range(2)], wscr,
        )

    keep = (lanes((ROWS_LOC, 256)) % 128) < BW
    squares = jnp.zeros((16, 128), jnp.float32)
    for j in range(PER):
        g = i * PER + j
        y = rotate_group(
            pair, g * 4, x_ref[:, 256 * j : 256 * j + 256],
            [rot_ref[0, 2 * j + c] for c in range(2)],
            [rot_ref[1, 2 * j + c] for c in range(2)], wscr,
        )
        out = jnp.where(keep, y, carry[...])
        carry[...] = y
        out_ref[:, 256 * j : 256 * j + 256] = out
        if with_gram:
            squares = group_gram(pair_next, g * 4, out, j, gscr, pay_ref, squares)
    if with_gram:
        put_squares(squares, pay_ref)


def apply_call(pair, pair_next, x, rot, with_gram):
    out_shape = [jax.ShapeDtypeStruct(x.shape, jnp.bfloat16)]
    out_specs = [pl.BlockSpec((ROWS_LOC, WIDE), lambda i, p, q: (0, i))]
    scratch = [pltpu.VMEM((256, 256), jnp.bfloat16), pltpu.VMEM((ROWS_LOC, 256), jnp.bfloat16)]
    if with_gram:
        out_shape.append(jax.ShapeDtypeStruct((2, CHUNKS, PAY, 128), jnp.bfloat16))
        out_specs.append(pl.BlockSpec((2, 1, PAY, 128), lambda i, p, q: (0, i, 0, 0)))
        scratch.append(pltpu.VMEM((256, 256), jnp.float32))
    return pl.pallas_call(
        functools.partial(apply_body, with_gram),
        out_shape=out_shape,
        grid_spec=pltpu.PrefetchScalarGridSpec(
            num_scalar_prefetch=2,
            grid=(CHUNKS,),
            in_specs=[
                pl.BlockSpec((ROWS_LOC, WIDE), lambda i, p, q: (0, i)),
                pl.BlockSpec((2, NZ, BW, 128), lambda i, p, q: (0, i, 0, 0)),
                pl.BlockSpec((ROWS_LOC, 256), lambda i, p, q: (0, GROUPS - 1)),
                pl.BlockSpec((2, 2, BW, 128), lambda i, p, q: (0, GROUPS - 1, 0, 0)),
            ],
            out_specs=out_specs,
            scratch_shapes=scratch,
        ),
    )(pair, pair_next, x, rot, x, rot)


def half_rotation(own0, own1, squares, core):
    raw = jnp.concatenate(
        [own0[:, :BW], own0[:, BW:], own1[:, :BW], own1[:, BW:]], axis=0
    )
    scale = 1.0 / jnp.sqrt(squares + 1e-06)
    row = lax.broadcasted_iota(jnp.int32, (BW, BW), 0)
    col = lax.broadcasted_iota(jnp.int32, (BW, BW), 1)
    eye = row == col
    left_scale = jnp.sum(jnp.where(eye, scale[:, :BW], 0.0), axis=1, keepdims=True)
    cross = 0.5 * raw * left_scale * scale[:, BW:]
    crossed = cross.T
    is_left = core == 0
    y = jnp.where(is_left, cross, crossed)
    yt = jnp.where(is_left, crossed, cross)
    unit = jnp.where(eye, 1.0, 0.0)
    full = unit + jnp.dot(y, yt, precision=HIGH, preferred_element_type=jnp.float32)
    m = jnp.concatenate([full, unit], axis=1)
    below = lax.broadcasted_iota(jnp.int32, (BW, 1), 0)
    pivots = None
    for k in range(BW):
        pivot_row = m[k : k + 1, :]
        inverse = 1.0 / m[k : k + 1, k : k + 1]
        factor = jnp.where(below > k, m[:, k : k + 1], 0.0) * inverse
        m = m - factor * pivot_row
    diag = jnp.sum(jnp.where(eye, m[:, :BW], 0.0), axis=1, keepdims=True)
    lower = m[:, BW:] * lax.rsqrt(diag)
    upper = lower.T
    other = jnp.dot(yt, upper, precision=HIGH, preferred_element_type=jnp.float32)
    first = upper
    second = jnp.where(is_left, -other, other)
    return jnp.concatenate([first, second], axis=1).astype(jnp.bfloat16)


def comm_body(pay, out, got0, sent1, got1, sent2, got2, *sems):
    (ss0, rs0, ss1, rs1, ss2, rs2, ss4, rs4, ss5, rs5, ss6, rs6, ss7, rs7) = sems
    row, blk = lax.axis_index("row"), lax.axis_index("blk")
    core = lax.rem(row, 2)
    z = lax.rem(blk, NZ)
    x = (row // 2) * XL + lax.rem(blk // NZ, XL)
    y = blk // (NZ * XL)
    sibling = 1 - core

    def device(x, y, z, core):
        return {"row": (x // XL) * 2 + core, "blk": (y * XL + lax.rem(x, XL)) * NZ + z}

    def ahead(v, d, n):
        return lax.rem(v + d, n)

    def behind(v, d, n):
        return lax.rem(v + (n - d), n)

    own = x * NY + y
    own_pos = own * NZ + z
    pending = []

    def send(src, dst, send_sem, recv_sem, target):
        copy = pltpu.make_async_remote_copy(
            src_ref=src, dst_ref=dst, send_sem=send_sem, recv_sem=recv_sem,
            device_id=target, device_id_type=MESH,
        )
        copy.start()
        pending.append(copy)

    def arrived(dst, send_sem, recv_sem):
        pltpu.make_async_remote_copy(
            src_ref=dst, dst_ref=dst, send_sem=send_sem, recv_sem=recv_sem,
            device_id=device(x, y, z, sibling), device_id_type=MESH,
        ).wait_recv()

    def plane(d):
        there = ahead(own, d, CHUNKS)
        return there // NY, lax.rem(there, NY)

    barrier = pltpu.get_barrier_semaphore()
    greeted = [device(*plane(d), z, core) for d in range(1, CHUNKS)]
    greeted += [
        device(x, y, ahead(z, dz, NZ), ahead(core, dc, 2))
        for dz in range(NZ) for dc in range(2) if dz or dc
    ]
    for peer in greeted:
        pl.semaphore_signal(barrier, inc=1, device_id=peer, device_id_type=MESH)
    pl.semaphore_wait(barrier, len(greeted))

    order = list(range(1, CHUNKS)) + [0]
    for d in order:
        send(pay.at[sibling, ahead(own, d, CHUNKS)], got0.at[d], ss0.at[d], rs0.at[d],
             device(x, y, z, sibling))
    for d in order:
        arrived(got0.at[d], ss0.at[d], rs0.at[d])
        both = pay[core, ahead(own, d, CHUNKS)].astype(jnp.float32) + got0[d].astype(jnp.float32)
        if d == 0:
            total = both
        else:
            sent1[d] = both.astype(jnp.bfloat16)
            send(sent1.at[d], got1.at[d], ss1.at[d], rs1.at[d], device(*plane(d), z, core))
    for d in range(1, CHUNKS):
        arrived(got1.at[d], ss1.at[d], rs1.at[d])
        total = total + got1[d].astype(jnp.float32)
    for there in range(NZ):
        sent2[there, :16] = total[16 * there : 16 * there + 16]
        sent2[there, 16:] = total[CROSS_ROWS : CROSS_ROWS + 8]
    for dz in range(NZ):
        for dc in range(2):
            if dz or dc:
                there = ahead(z, dz, NZ)
                send(sent2.at[there], got2.at[core, dz], ss2.at[dc, dz], rs2.at[dc, dz],
                     device(x, y, there, ahead(core, dc, 2)))
    got2[core, 0] = sent2[z]
    for dz in range(NZ):
        for dc in range(2):
            if dz or dc:
                arrived(got2.at[ahead(core, dc, 2), dz], ss2.at[dc, dz], rs2.at[dc, dz])
    halves = [sum([got2[h, dz] for dz in range(1, NZ)], got2[h, 0]) for h in range(2)]
    pick = lax.broadcasted_iota(jnp.int32, (8, 128), 0) == z
    squares = jnp.sum(jnp.where(pick, halves[0][16:], 0.0), axis=0, keepdims=True)
    out[core, own_pos] = half_rotation(halves[0][:16], halves[1][:16], squares, core)

    for dz in range(1, NZ):
        send(out.at[core, own_pos], out.at[core, own_pos], ss4.at[dz], rs4.at[dz],
             device(x, y, ahead(z, dz, NZ), core))
    for dz in range(1, NZ):
        arrived(out.at[core, own * NZ + behind(z, dz, NZ)], ss4.at[dz], rs4.at[dz])

    def block(which, e, f):
        bx = behind(x, which * e + (1 - which) * f, NX)
        by = behind(y, (1 - which) * e + which * f, NY)
        return out.at[which, pl.ds((bx * NY + by) * NZ, NZ)]

    def along(e, f):
        return device(
            ahead(x, core * e + (1 - core) * f, NX), ahead(y, (1 - core) * e + core * f, NY),
            z, core,
        )

    def forward(e, f):
        send(block(core, e, f), block(core, e, f), ss7.at[e, f], rs7.at[e, f],
             device(x, y, z, sibling))

    for e in range(1, NX):
        send(block(core, 0, 0), block(core, 0, 0), ss5.at[e], rs5.at[e], along(e, 0))
    for e in range(NX):
        if e:
            arrived(block(core, e, 0), ss5.at[e], rs5.at[e])
        for f in range(1, NX):
            send(block(core, e, 0), block(core, e, 0), ss6.at[e, f], rs6.at[e, f], along(0, f))
        forward(e, 0)
    for e in range(NX):
        for f in range(1, NX):
            arrived(block(core, e, f), ss6.at[e, f], rs6.at[e, f])
            forward(e, f)
    for e in range(NX):
        for f in range(NX):
            arrived(block(sibling, e, f), ss7.at[e, f], rs7.at[e, f])
    for copy in pending:
        copy.wait_send()


def exchange(pay):
    dma = pltpu.SemaphoreType.DMA
    shapes = [(CHUNKS,), (CHUNKS,), (2, NZ), (NZ,), (NX,), (NX, NX), (NX, NX)]
    return pl.pallas_call(
        comm_body,
        out_shape=jax.ShapeDtypeStruct((2, COUPLES, BW, 128), jnp.bfloat16),
        in_specs=[pl.BlockSpec(memory_space=pltpu.VMEM)],
        out_specs=pl.BlockSpec(memory_space=pltpu.VMEM),
        scratch_shapes=[
            pltpu.VMEM((CHUNKS, PAY, 128), jnp.bfloat16),
            pltpu.VMEM((CHUNKS, PAY, 128), jnp.bfloat16),
            pltpu.VMEM((CHUNKS, PAY, 128), jnp.bfloat16),
            pltpu.VMEM((NZ, 24, 128), jnp.float32),
            pltpu.VMEM((2, NZ, 24, 128), jnp.float32),
        ]
        + [dma(shape) for shape in shapes for _ in range(2)],
        compiler_params=pltpu.CompilerParams(
            collective_id=0, has_side_effects=True, vmem_limit_bytes=32 * 2**20
        ),
    )(pay)


def local(matrix, pairing):
    flat = pairing.reshape(STEPS, GROUPS * 4)
    pay = gram_call(flat[0], matrix)
    rot = exchange(pay)
    current, pay = apply_call(flat[0], flat[1], matrix, rot, True)
    rot = exchange(pay)
    return apply_call(flat[1], flat[1], current, rot, False)[0]


def solution(mesh):
    placed = (P(("row", "blk"), None), P())
    return jax.shard_map(
        local, mesh=mesh, in_specs=placed, out_specs=P(("row", "blk"), None), check_vma=False
    )
```

```python
import jax
import jax.numpy as jnp
from jax import lax
from jax.experimental import pallas as pl
from jax.experimental.pallas import tpu as pltpu
from jax.sharding import PartitionSpec as P

BW = 64
STEPS = 2
XH, XL, NY, NZ = 2, 2, 4, 8
NX = XH * XL
CHUNKS = NX * NY
PER = NZ // 2
GROUPS = CHUNKS * PER
ROWS_LOC = 192
CROSS_ROWS = 32 * PER
PAY = CROSS_ROWS + 16
WIDE = 256 * PER
LAG = 2
HIGH = lax.Precision.HIGHEST
MESH = pl.DeviceIdType.MESH
ORDER = [(0, 0), (1, 0), (3, 0), (0, 1), (0, 3), (1, 1), (3, 3), (1, 3), (3, 1),
         (2, 0), (0, 2), (2, 1), (1, 2), (2, 3), (3, 2), (2, 2)]


def lanes(shape):
    return lax.broadcasted_iota(jnp.int32, shape, len(shape) - 1)


def gram_of(xg):
    return lax.dot_general(
        xg, xg, (((0,), (0,)), ((), ())), preferred_element_type=jnp.float32
    )


def group_payload(slots, j, gscr):
    row = lax.broadcasted_iota(jnp.int32, (BW, 128), 0)
    lane = lanes((BW, 128))
    sq = []
    for t in range(2):
        tile = slice(128 * t, 128 * t + 128)
        first = jnp.where(lane == row, gscr[j, 128 * t : 128 * t + BW, tile], 0.0)
        second = jnp.where(lane == row + BW, gscr[j, 128 * t + BW : 128 * t + 128, tile], 0.0)
        sq.append(jnp.sum(first + second, axis=0, keepdims=True))
    turned_sq = [pltpu.roll(v, BW, 1) for v in sq]
    lane32 = lanes((32, 128)) < BW
    lane1 = lanes((1, 128)) < BW
    cross, squares = [], []
    for c in range(2):
        a, b = slots[2 * c], slots[2 * c + 1]
        high_b = jnp.broadcast_to(b >= 2, (BW, 128))
        tile = None
        for s in range(4):
            rows = slice(BW * s, BW * s + BW)
            part = jnp.where(high_b, gscr[j, rows, 128:], gscr[j, rows, :128])
            tile = part if tile is None else jnp.where(
                jnp.broadcast_to(a == s, (BW, 128)), part, tile
            )
        turned = pltpu.roll(tile, BW, 1)
        odd_b = (b == 1) | (b == 3)
        odd = jnp.broadcast_to(odd_b, (32, 128))
        low = jnp.where(odd, turned[:32], tile[:32])
        high = jnp.where(odd, tile[32:], turned[32:])
        cross.append(jnp.where(lane32, low, high).astype(jnp.bfloat16))
        sa = jnp.where(a == 0, sq[0], jnp.where(
            a == 1, turned_sq[0], jnp.where(a == 2, sq[1], turned_sq[1])))
        sb = jnp.where(b == 0, turned_sq[0], jnp.where(
            b == 1, sq[0], jnp.where(b == 2, turned_sq[1], sq[1])))
        squares.append(jnp.where(lane1, sa, sb))
    return cross, squares


def rotate_group(slots, xg, left, right):
    lane = lanes((BW, 128)) < BW
    zero = jnp.zeros((BW, 128), jnp.bfloat16)
    tiles = []
    for c in range(2):
        a, b = [jnp.broadcast_to(slots[2 * c + k], (BW, 128)) for k in range(2)]
        top = jnp.where(lane, left[c], right[c])
        bot = pltpu.roll(jnp.where(lane, right[c], left[c]), BW, 1)
        tiles.append(jnp.concatenate(
            [jnp.where(a == s, top, jnp.where(b == s, bot, zero)) for s in range(4)], axis=0
        ))
    return jnp.dot(
        xg, jnp.concatenate(tiles, axis=1), preferred_element_type=jnp.float32
    ).astype(jnp.bfloat16)


def half_rotations(packed, squares):
    raw = jnp.concatenate([packed[:, :BW], packed[:, BW:]], axis=0)
    scale = 1.0 / jnp.sqrt(squares + 1e-06)
    row = lax.broadcasted_iota(jnp.int32, (BW, BW), 0)
    col = lax.broadcasted_iota(jnp.int32, (BW, BW), 1)
    eye = row == col
    left_scale = jnp.sum(jnp.where(eye, scale[:, :BW], 0.0), axis=1, keepdims=True)
    cross = 0.5 * raw * left_scale * scale[:, BW:]
    crossed = cross.T
    unit = jnp.where(eye, 1.0, 0.0)
    below = lax.broadcasted_iota(jnp.int32, (BW, 1), 0)
    pairs = [(cross, crossed), (crossed, cross)]
    work = [
        jnp.concatenate(
            [unit + jnp.dot(u, v, precision=HIGH, preferred_element_type=jnp.float32), unit],
            axis=1,
        )
        for u, v in pairs
    ]
    for k in range(BW):
        for side in range(2):
            m = work[side]
            inverse = 1.0 / m[k : k + 1, k : k + 1]
            factor = jnp.where(below > k, m[:, k : k + 1], 0.0)
            work[side] = m - factor * (m[k : k + 1, :] * inverse)
    halves = []
    for side in range(2):
        m = work[side]
        diag = jnp.sum(jnp.where(eye, m[:, :BW], 0.0), axis=1, keepdims=True)
        upper = (m[:, BW:] * lax.rsqrt(diag)).T
        other = jnp.dot(
            pairs[side][1], upper, precision=HIGH, preferred_element_type=jnp.float32
        )
        halves.append(jnp.concatenate([upper, other if side else -other], axis=1))
    return [half.astype(jnp.bfloat16) for half in halves]


def body(pair, matrix, out, cur, gscr, pay, got0, sent1, got1, sent2, got2, rot, *sems):
    (ins, ss0, rs0, ss1, rs1, ss2, rs2, ss4, rs4, ss5, rs5, ss6, rs6, ss7, rs7, outs, edges) = sems
    row, blk = lax.axis_index("row"), lax.axis_index("blk")
    core = lax.rem(row, 2)
    z = lax.rem(blk, NZ)
    x = (row // 2) * XL + lax.rem(blk // NZ, XL)
    y = blk // (NZ * XL)
    sibling = 1 - core
    own = x * NY + y
    mine = z // 2
    owner = lax.rem(z, 2) == core

    def device(x, y, z, core):
        return {"row": (x // XL) * 2 + core, "blk": (y * XL + lax.rem(x, XL)) * NZ + z}

    beside = device(x, y, z, sibling)

    def ahead(v, d, n):
        return lax.rem(v + d, n)

    def behind(v, d, n):
        return lax.rem(v + (n - d), n)

    def plane(d):
        there = ahead(own, d, CHUNKS)
        return device(there // NY, lax.rem(there, NY), z, core)

    def copy(src, dst, send_sem, recv_sem, target):
        return pltpu.make_async_remote_copy(
            src_ref=src, dst_ref=dst, send_sem=send_sem, recv_sem=recv_sem,
            device_id=target, device_id_type=MESH,
        )

    def columns(chunk, first=0, count=WIDE):
        return pl.ds(pl.multiple_of(chunk * WIDE + first, 256), count)

    def load(s):
        at = columns(ahead(own, s + 1, CHUNKS))
        return pltpu.make_async_copy(matrix.at[:, at], cur.at[0, :, at], ins.at[s])

    @pl.loop(0, CHUNKS)
    def _(s):
        load(s).start()

    barrier = pltpu.get_barrier_semaphore()
    greeted = [plane(d) for d in range(1, CHUNKS)] + [beside]
    greeted += [device(x, y, ahead(z, dz, NZ), core) for dz in range(1, NZ)]
    for peer in greeted:
        pl.semaphore_signal(barrier, inc=1, device_id=peer, device_id_type=MESH)
    pl.semaphore_wait(barrier, len(greeted))

    def turn(t):
        src, dst = t % 2, (t + 1) % 2

        def slots_of(chunk):
            numbers = pair[pl.ds(t * CHUNKS + chunk, 1), :]
            return [
                [jnp.broadcast_to(numbers[:, n : n + 1], (1, 128)) for n in range(4 * j, 4 * j + 4)]
                for j in range(PER)
            ]

        def core_copy(s):
            return copy(pay.at[t, s, sibling], got0.at[t, s], ss0.at[t, s], rs0.at[t, s], beside)

        def plane_copy(s):
            return copy(sent1.at[t, s], got1.at[t, s], ss1.at[t, s], rs1.at[t, s], plane(s + 1))

        def summed(s):
            core_copy(s).wait_recv()
            return pay[t, s, core].astype(jnp.float32) + got0[t, s].astype(jnp.float32)

        def pass_on(s):
            sent1[t, s] = summed(s).astype(jnp.bfloat16)
            plane_copy(s).start()

        @pl.loop(0, CHUNKS)
        def _(s):
            chunk = ahead(own, s + 1, CHUNKS)
            if t == 0:
                load(s).wait()
            for j in range(PER):
                at = pl.ds(pl.multiple_of(chunk * WIDE + 256 * j, 256), 256)
                gscr[j] = gram_of(cur[src, :, at])
            slots = slots_of(chunk)
            row16 = lax.broadcasted_iota(jnp.int32, (16, 128), 0)
            squares = [jnp.zeros((16, 128), jnp.float32)] * 2
            for j in range(PER):
                cross, sq = group_payload(slots[j], j, gscr)
                for c in range(2):
                    pay[t, s, c, 32 * j : 32 * j + 32] = cross[c]
                    squares[c] = jnp.where(row16 == j, sq[c], squares[c])
            for c in range(2):
                pay[t, s, c, CROSS_ROWS:] = squares[c].astype(jnp.bfloat16)
            core_copy(s).start()

            @pl.when(s >= LAG)
            def _():
                pass_on(s - LAG)

        @pl.loop(CHUNKS - LAG, CHUNKS - 1)
        def _(s):
            pass_on(s)

        total = summed(CHUNKS - 1)
        for s in range(CHUNKS - 1):
            plane_copy(s).wait_recv()
            total = total + got1[t, s].astype(jnp.float32)

        for j in range(PER):
            sent2[t, j, :32] = total[32 * j : 32 * j + 32]
            sent2[t, j, 32:] = total[CROSS_ROWS : CROSS_ROWS + 8]

        def sum_copy(dz):
            there = ahead(z, dz, NZ)
            return copy(sent2.at[t, there // 2], got2.at[t, dz], ss2.at[t, dz], rs2.at[t, dz],
                        device(x, y, there, core))

        def gather_copy(dz, at):
            piece = rot.at[t, core, own, at]
            return copy(piece, piece, ss4.at[t, dz], rs4.at[t, dz],
                        device(x, y, ahead(z, dz, NZ), core))

        @pl.when(owner)
        def _():
            for dz in range(2, NZ, 2):
                sum_copy(dz).start()
            got = sent2[t, mine]
            for dz in range(1, NZ):
                sum_copy(dz).wait_recv()
                got = got + got2[t, dz]
            pick = lax.broadcasted_iota(jnp.int32, (8, 128), 0) == mine
            squares = jnp.sum(jnp.where(pick, got[32:], 0.0), axis=0, keepdims=True)
            halves = half_rotations(got[:32], squares)
            for side in range(2):
                rot[t, core, own, mine, side] = halves[side]
            for dz in range(1, NZ):
                gather_copy(dz, mine).start()
            for dz in range(2, NZ, 2):
                gather_copy(dz, behind(z, dz, NZ) // 2).wait_recv()
            for dz in range(2, NZ, 2):
                sum_copy(dz).wait_send()
            for dz in range(1, NZ):
                gather_copy(dz, mine).wait_send()

        @pl.when(jnp.logical_not(owner))
        def _():
            for dz in range(1, NZ, 2):
                sum_copy(dz).start()
            for dz in range(1, NZ, 2):
                gather_copy(dz, behind(z, dz, NZ) // 2).wait_recv()
            for dz in range(1, NZ, 2):
                sum_copy(dz).wait_send()

        def where(e, f):
            bx = behind(x, core * e + (1 - core) * f, NX)
            by = behind(y, (1 - core) * e + core * f, NY)
            return bx * NY + by

        def block(which, e, f, part=None):
            piece = rot.at[t, which, where(e, f)]
            return piece if part is None else piece.at[pl.ds(part * (PER // 2), PER // 2)]

        def along(e, f):
            return device(
                ahead(x, core * e + (1 - core) * f, NX),
                ahead(y, (1 - core) * e + core * f, NY), z, core,
            )

        def first_copy(e):
            return copy(block(core, 0, 0), block(core, 0, 0), ss5.at[t, e], rs5.at[t, e],
                        along(e, 0))

        def second_copy(e, f):
            piece = block(core, e, 0)
            return copy(piece, piece, ss6.at[t, e, f], rs6.at[t, e, f], along(0, f))

        def second_wait(e, f):
            piece = block(core, e, f)
            copy(piece, piece, ss6.at[t, e, f], rs6.at[t, e, f], beside).wait_recv()

        def relay_copy(e, f):
            piece = block(core, e, f, f // 2)
            k = f - f // 2 * 3
            return copy(piece, piece, ss6.at[t, e, 2 * k], rs6.at[t, e, 2 * k], along(0, f))

        def relay_wait(e, f):
            piece = block(core, e, 2, f // 2)
            k = f - f // 2 * 3
            copy(piece, piece, ss6.at[t, e, 2 * k], rs6.at[t, e, 2 * k], beside).wait_recv()

        def to_core(e, f):
            piece = block(core, e, f)
            return copy(piece, piece, ss7.at[t, e, f], rs7.at[t, e, f], beside)

        def core_wait(e, f):
            piece = block(sibling, e, f)
            copy(piece, piece, ss7.at[t, f, e], rs7.at[t, f, e], beside).wait_recv()

        for e in range(1, NX):
            first_copy(e).start()
        for e in (0, 1, 3, 2):
            if e:
                piece = block(core, e, 0)
                copy(piece, piece, ss5.at[t, e], rs5.at[t, e], beside).wait_recv()
            second_copy(e, 1).start()
            second_copy(e, 3).start()
            to_core(e, 0).start()

        def relay(e):
            for f in (1, 3):
                second_wait(e, f)
                relay_copy(e, f).start()
                to_core(e, f).start()

        def last(e):
            relay_wait(e, 1)
            relay_wait(e, 3)
            to_core(e, 2).start()

        events = {0: [(relay, 0)], 1: [(relay, 1)], 3: [(relay, 3)], 5: [(relay, 2)],
                  8: [(last, 0), (last, 1)], 9: [(last, 3), (last, 2)]}

        def out_copy(k):
            e, f = nth(k)
            at = columns(where(e, f), 256, WIDE - 256)
            return pltpu.make_async_copy(cur.at[dst, :, at], out.at[:, at], outs.at[k])

        def edge_copy(i):
            at = columns(i, 0, 256)
            return pltpu.make_async_copy(cur.at[dst, :, at], out.at[:, at], edges.at[i])

        def nth(k):
            e = sum(jnp.where(k == n, v[0], 0) for n, v in enumerate(ORDER) if v[0])
            f = sum(jnp.where(k == n, v[1], 0) for n, v in enumerate(ORDER) if v[1])
            return e, f

        keep = lax.rem(lanes((ROWS_LOC, 256)), 128) < BW

        @pl.loop(0, CHUNKS)
        def _(k):
            for n, steps in events.items():
                @pl.when(k == n)
                def _():
                    for step, e in steps:
                        step(e)

            e, f = nth(k)
            core_wait(e, f)
            chunk = where(e, f)
            slots = slots_of(chunk)
            before = None
            for j in range(PER):
                at = pl.ds(pl.multiple_of(chunk * WIDE + 256 * j, 256), 256)
                now = rotate_group(
                    slots[j], cur[src, :, at],
                    [rot[t, c, chunk, j, 0] for c in range(2)],
                    [rot[t, c, chunk, j, 1] for c in range(2)],
                )
                odd = cur[dst, :, at] if before is None else before
                cur[dst, :, at] = jnp.where(keep, now, odd)
                before = now
            at = columns(ahead(chunk, 1, CHUNKS), 0, 256)
            cur[dst, :, at] = jnp.where(keep, cur[dst, :, at], before)
            if t == STEPS - 1:
                out_copy(k).start()

        if t == STEPS - 1:
            @pl.loop(0, CHUNKS)
            def _(i):
                edge_copy(i).start()

            @pl.loop(0, CHUNKS)
            def _(i):
                out_copy(i).wait()
                edge_copy(i).wait()

        @pl.loop(0, CHUNKS)
        def _(s):
            core_copy(s).wait_send()

        @pl.loop(0, CHUNKS - 1)
        def _(s):
            plane_copy(s).wait_send()

        for e in range(1, NX):
            first_copy(e).wait_send()

        @pl.loop(0, NX)
        def _(e):
            for f in (1, 3):
                second_copy(e, f).wait_send()
                relay_copy(e, f).wait_send()
            for f in range(NX):
                to_core(e, f).wait_send()

    for t in range(STEPS):
        turn(t)


def local(matrix, pairing):
    dma = pltpu.SemaphoreType.DMA
    shapes = [(CHUNKS,), (CHUNKS,), (NZ,), (NZ,), (NX,), (NX, 5), (NX, NX)]
    vmem = pltpu.VMEM
    return pl.pallas_call(
        body,
        out_shape=jax.ShapeDtypeStruct(matrix.shape, matrix.dtype),
        in_specs=[pl.BlockSpec(memory_space=pltpu.VMEM), pl.BlockSpec(memory_space=pl.ANY)],
        out_specs=pl.BlockSpec(memory_space=pl.ANY),
        scratch_shapes=[
            vmem((2, ROWS_LOC, 256 * GROUPS), jnp.bfloat16),
            vmem((PER, 256, 256), jnp.float32),
            vmem((STEPS, CHUNKS, 2, PAY, 128), jnp.bfloat16),
            vmem((STEPS, CHUNKS, PAY, 128), jnp.bfloat16),
            vmem((STEPS, CHUNKS - 1, PAY, 128), jnp.bfloat16),
            vmem((STEPS, CHUNKS - 1, PAY, 128), jnp.bfloat16),
            vmem((STEPS, PER, 40, 128), jnp.float32),
            vmem((STEPS, NZ, 40, 128), jnp.float32),
            vmem((STEPS, 2, CHUNKS, PER, 2, BW, 128), jnp.bfloat16),
        ]
        + [dma((CHUNKS,))]
        + [dma((STEPS,) + shape) for shape in shapes for _ in range(2)]
        + [dma((CHUNKS,))] * 2,
        compiler_params=pltpu.CompilerParams(
            collective_id=0, has_side_effects=True, vmem_limit_bytes=48 * 2**20
        ),
    )(pairing.reshape(STEPS * CHUNKS, 4 * PER), matrix)


def solution(mesh):
    placed = (P(("row", "blk"), None), P())
    return jax.shard_map(
        local, mesh=mesh, in_specs=placed, out_specs=P(("row", "blk"), None), check_vma=False
    )
```

```python
import jax
import jax.numpy as jnp
from jax import lax
from jax.experimental import pallas as pl
from jax.experimental.pallas import tpu as pltpu
from jax.sharding import PartitionSpec as P

BW = 64
STEPS = 2
XH, XL, NY, NZ = 2, 2, 4, 8
NX = XH * XL
CHUNKS = NX * NY
PER = NZ // 2
GROUPS = CHUNKS * PER
ROWS_LOC = 192
CROSS_ROWS = 32 * PER
PAY = CROSS_ROWS + 16
WIDE = 256 * PER
LAG = 2
HIGH = lax.Precision.HIGHEST
MESH = pl.DeviceIdType.MESH
ORDER = [(0, 0), (0, 1), (0, 3), (1, 0), (3, 0), (1, 1), (1, 3), (3, 1), (3, 3),
         (0, 2), (2, 0), (1, 2), (2, 1), (3, 2), (2, 3), (2, 2)]


def lanes(shape):
    return lax.broadcasted_iota(jnp.int32, shape, len(shape) - 1)


def gram_of(xg):
    return lax.dot_general(
        xg, xg, (((0,), (0,)), ((), ())), preferred_element_type=jnp.float32
    )


def group_payload(slots, j, gscr):
    row = lax.broadcasted_iota(jnp.int32, (BW, 128), 0)
    lane = lanes((BW, 128))
    sq = []
    for t in range(2):
        tile = slice(128 * t, 128 * t + 128)
        first = jnp.where(lane == row, gscr[j, 128 * t : 128 * t + BW, tile], 0.0)
        second = jnp.where(lane == row + BW, gscr[j, 128 * t + BW : 128 * t + 128, tile], 0.0)
        sq.append(jnp.sum(first + second, axis=0, keepdims=True))
    turned_sq = [pltpu.roll(v, BW, 1) for v in sq]
    lane32 = lanes((32, 128)) < BW
    lane1 = lanes((1, 128)) < BW
    cross, squares = [], []
    for c in range(2):
        a, b = slots[2 * c], slots[2 * c + 1]
        high_b = jnp.broadcast_to(b >= 2, (BW, 128))
        tile = None
        for s in range(4):
            rows = slice(BW * s, BW * s + BW)
            part = jnp.where(high_b, gscr[j, rows, 128:], gscr[j, rows, :128])
            tile = part if tile is None else jnp.where(
                jnp.broadcast_to(a == s, (BW, 128)), part, tile
            )
        turned = pltpu.roll(tile, BW, 1)
        odd_b = (b == 1) | (b == 3)
        odd = jnp.broadcast_to(odd_b, (32, 128))
        low = jnp.where(odd, turned[:32], tile[:32])
        high = jnp.where(odd, tile[32:], turned[32:])
        cross.append(jnp.where(lane32, low, high).astype(jnp.bfloat16))
        sa = jnp.where(a == 0, sq[0], jnp.where(
            a == 1, turned_sq[0], jnp.where(a == 2, sq[1], turned_sq[1])))
        sb = jnp.where(b == 0, turned_sq[0], jnp.where(
            b == 1, sq[0], jnp.where(b == 2, turned_sq[1], sq[1])))
        squares.append(jnp.where(lane1, sa, sb))
    return cross, squares


def rotate_group(slots, xg, left, right):
    lane = lanes((BW, 128)) < BW
    zero = jnp.zeros((BW, 128), jnp.bfloat16)
    tiles = []
    for c in range(2):
        a, b = [jnp.broadcast_to(slots[2 * c + k], (BW, 128)) for k in range(2)]
        top = jnp.where(lane, left[c], right[c])
        bot = pltpu.roll(jnp.where(lane, right[c], left[c]), BW, 1)
        tiles.append(jnp.concatenate(
            [jnp.where(a == s, top, jnp.where(b == s, bot, zero)) for s in range(4)], axis=0
        ))
    return jnp.dot(
        xg, jnp.concatenate(tiles, axis=1), preferred_element_type=jnp.float32
    ).astype(jnp.bfloat16)


def half_rotations(packed, squares):
    raw = jnp.concatenate([packed[:, :BW], packed[:, BW:]], axis=0)
    scale = 1.0 / jnp.sqrt(squares + 1e-06)
    row = lax.broadcasted_iota(jnp.int32, (BW, BW), 0)
    col = lax.broadcasted_iota(jnp.int32, (BW, BW), 1)
    eye = row == col
    left_scale = jnp.sum(jnp.where(eye, scale[:, :BW], 0.0), axis=1, keepdims=True)
    cross = 0.5 * raw * left_scale * scale[:, BW:]
    crossed = cross.T
    unit = jnp.where(eye, 1.0, 0.0)
    number = lax.broadcasted_iota(jnp.int32, (BW, 1), 0)
    pairs = [(cross, crossed), (crossed, cross)]
    work = [
        jnp.concatenate(
            [unit + jnp.dot(u, v, precision=HIGH, preferred_element_type=jnp.float32), unit],
            axis=1,
        )
        for u, v in pairs
    ]
    for k in range(0, BW - 2, 2):
        for side in range(2):
            m = work[side]
            p, q, r = [
                jnp.broadcast_to(m[i : i + 1, j : j + 1], (1, 128))
                for i, j in ((k, k), (k, k + 1), (k + 1, k + 1))
            ]
            inverse = 1.0 / (p * r - q * q)
            over, under = m[k : k + 1, :], m[k + 1 : k + 2, :]
            one = (r * over - q * under) * inverse
            two = (p * under - q * over) * inverse
            below = number > k + 1
            work[side] = m - (
                jnp.where(below, m[:, k : k + 1], 0.0) * one
                + jnp.where(below, m[:, k + 1 : k + 2], 0.0) * two
            )
    for side in range(2):
        m = work[side]
        pivot = jnp.sum(jnp.where(eye, m[:, :BW], 0.0), axis=1, keepdims=True)
        beside = jnp.sum(jnp.where(row == col + 1, m[:, :BW], 0.0), axis=1, keepdims=True)
        above = pltpu.roll(jnp.broadcast_to(pivot, (BW, 128)), 1, 0)
        odd = jnp.where(lax.rem(number, 2) == 1, beside, 0.0)
        work[side] = m - odd / above * pltpu.roll(m, 1, 0)
    halves = []
    for side in range(2):
        m = work[side]
        diag = jnp.sum(jnp.where(eye, m[:, :BW], 0.0), axis=1, keepdims=True)
        upper = (m[:, BW:] * lax.rsqrt(diag)).T
        other = jnp.dot(
            pairs[side][1], upper, precision=HIGH, preferred_element_type=jnp.float32
        )
        halves.append(jnp.concatenate([upper, other if side else -other], axis=1))
    return [half.astype(jnp.bfloat16) for half in halves]


def body(pair, matrix, out, cur, gscr, pay, got0, sent1, got1, sent2, got2, rot, *sems):
    (ins, ss0, rs0, ss1, rs1, ss2, rs2, ss4, rs4, ss5, rs5, ss6, rs6, ss7, rs7) = sems
    row, blk = lax.axis_index("row"), lax.axis_index("blk")
    core = lax.rem(row, 2)
    z = lax.rem(blk, NZ)
    x = (row // 2) * XL + lax.rem(blk // NZ, XL)
    y = blk // (NZ * XL)
    sibling = 1 - core
    own = x * NY + y
    mine = z // 2
    owner = lax.rem(z, 2) == core

    def device(x, y, z, core):
        return {"row": (x // XL) * 2 + core, "blk": (y * XL + lax.rem(x, XL)) * NZ + z}

    beside = device(x, y, z, sibling)

    def ahead(v, d, n):
        return lax.rem(v + d, n)

    def behind(v, d, n):
        return lax.rem(v + (n - d), n)

    def plane(d):
        there = ahead(own, d, CHUNKS)
        return device(there // NY, lax.rem(there, NY), z, core)

    def copy(src, dst, send_sem, recv_sem, target):
        return pltpu.make_async_remote_copy(
            src_ref=src, dst_ref=dst, send_sem=send_sem, recv_sem=recv_sem,
            device_id=target, device_id_type=MESH,
        )

    def columns(chunk, first=0, count=WIDE):
        return pl.ds(pl.multiple_of(chunk * WIDE + first, 256), count)

    def load(s):
        at = columns(ahead(own, s + 1, CHUNKS))
        return pltpu.make_async_copy(matrix.at[:, at], cur.at[0, :, at], ins.at[s])

    @pl.loop(0, CHUNKS)
    def _(s):
        load(s).start()

    barrier = pltpu.get_barrier_semaphore()
    greeted = [plane(d) for d in range(1, CHUNKS)] + [beside]
    greeted += [device(x, y, ahead(z, dz, NZ), core) for dz in range(1, NZ)]
    for peer in greeted:
        pl.semaphore_signal(barrier, inc=1, device_id=peer, device_id_type=MESH)

    def turn(t):
        src, dst = cur.at[t], cur.at[1] if t == 0 else out

        def slots_of(chunk):
            numbers = pair[pl.ds(t * CHUNKS + chunk, 1), :]
            return [
                [jnp.broadcast_to(numbers[:, n : n + 1], (1, 128)) for n in range(4 * j, 4 * j + 4)]
                for j in range(PER)
            ]

        def core_copy(s):
            return copy(pay.at[t, s, sibling], got0.at[t, s], ss0.at[t, s], rs0.at[t, s], beside)

        def plane_copy(s):
            return copy(sent1.at[t, s], got1.at[t, s], ss1.at[t, s], rs1.at[t, s], plane(s + 1))

        def summed(s):
            core_copy(s).wait_recv()
            return pay[t, s, core].astype(jnp.float32) + got0[t, s].astype(jnp.float32)

        def pass_on(s):
            sent1[t, s] = summed(s).astype(jnp.bfloat16)
            plane_copy(s).start()

        @pl.loop(0, CHUNKS)
        def _(s):
            chunk = ahead(own, s + 1, CHUNKS)
            if t == 0:
                load(s).wait()
            for j in range(PER):
                at = pl.ds(pl.multiple_of(chunk * WIDE + 256 * j, 256), 256)
                gscr[j] = gram_of(src[:, at])
            slots = slots_of(chunk)
            row16 = lax.broadcasted_iota(jnp.int32, (16, 128), 0)
            squares = [jnp.zeros((16, 128), jnp.float32)] * 2
            for j in range(PER):
                cross, sq = group_payload(slots[j], j, gscr)
                for c in range(2):
                    pay[t, s, c, 32 * j : 32 * j + 32] = cross[c]
                    squares[c] = jnp.where(row16 == j, sq[c], squares[c])
            for c in range(2):
                pay[t, s, c, CROSS_ROWS:] = squares[c].astype(jnp.bfloat16)
            if t == 0:
                @pl.when(s == 0)
                def _():
                    pl.semaphore_wait(barrier, len(greeted))

            core_copy(s).start()

            @pl.when(s >= LAG)
            def _():
                pass_on(s - LAG)

        @pl.loop(CHUNKS - LAG, CHUNKS - 1)
        def _(s):
            pass_on(s)

        total = summed(CHUNKS - 1)
        for s in range(CHUNKS - 1):
            plane_copy(s).wait_recv()
            total = total + got1[t, s].astype(jnp.float32)

        for j in range(PER):
            sent2[t, j, :32] = total[32 * j : 32 * j + 32]
            sent2[t, j, 32:] = total[CROSS_ROWS : CROSS_ROWS + 8]

        def sum_copy(dz):
            there = ahead(z, dz, NZ)
            return copy(sent2.at[t, there // 2], got2.at[t, dz], ss2.at[t, dz], rs2.at[t, dz],
                        device(x, y, there, core))

        def gather_copy(dz, at):
            piece = rot.at[t, core, own, at]
            return copy(piece, piece, ss4.at[t, dz], rs4.at[t, dz],
                        device(x, y, ahead(z, dz, NZ), core))

        @pl.when(owner)
        def _():
            for dz in range(2, NZ, 2):
                sum_copy(dz).start()
            got = sent2[t, mine]
            for dz in range(1, NZ):
                sum_copy(dz).wait_recv()
                got = got + got2[t, dz]
            pick = lax.broadcasted_iota(jnp.int32, (8, 128), 0) == mine
            squares = jnp.sum(jnp.where(pick, got[32:], 0.0), axis=0, keepdims=True)
            halves = half_rotations(got[:32], squares)
            for side in range(2):
                rot[t, core, own, mine, side] = halves[side]
            for dz in range(1, NZ):
                gather_copy(dz, mine).start()
            for dz in range(2, NZ, 2):
                gather_copy(dz, behind(z, dz, NZ) // 2).wait_recv()
            for dz in range(2, NZ, 2):
                sum_copy(dz).wait_send()
            for dz in range(1, NZ):
                gather_copy(dz, mine).wait_send()

        @pl.when(jnp.logical_not(owner))
        def _():
            for dz in range(1, NZ, 2):
                sum_copy(dz).start()
            for dz in range(1, NZ, 2):
                gather_copy(dz, behind(z, dz, NZ) // 2).wait_recv()
            for dz in range(1, NZ, 2):
                sum_copy(dz).wait_send()

        def where(e, f):
            bx = behind(x, core * e + (1 - core) * f, NX)
            by = behind(y, (1 - core) * e + core * f, NY)
            return bx * NY + by

        def block(which, e, f, part=None):
            piece = rot.at[t, which, where(e, f)]
            return piece if part is None else piece.at[pl.ds(part * (PER // 2), PER // 2)]

        def along(e, f):
            return device(
                ahead(x, core * e + (1 - core) * f, NX),
                ahead(y, (1 - core) * e + core * f, NY), z, core,
            )

        def first_copy(e):
            return copy(block(core, 0, 0), block(core, 0, 0), ss5.at[t, e], rs5.at[t, e],
                        along(e, 0))

        def second_copy(e, f):
            piece = block(core, e, 0)
            return copy(piece, piece, ss6.at[t, e, f], rs6.at[t, e, f], along(0, f))

        def second_wait(e, f):
            piece = block(core, e, f)
            copy(piece, piece, ss6.at[t, e, f], rs6.at[t, e, f], beside).wait_recv()

        def relay_copy(e, f):
            piece = block(core, e, f, f // 2)
            k = f - f // 2 * 3
            return copy(piece, piece, ss6.at[t, e, 2 * k], rs6.at[t, e, 2 * k], along(0, f))

        def relay_wait(e, f):
            piece = block(core, e, 2, f // 2)
            k = f - f // 2 * 3
            copy(piece, piece, ss6.at[t, e, 2 * k], rs6.at[t, e, 2 * k], beside).wait_recv()

        def to_core(e, f):
            piece = block(core, e, f)
            return copy(piece, piece, ss7.at[t, e, f], rs7.at[t, e, f], beside)

        def core_wait(e, f):
            piece = block(sibling, e, f)
            copy(piece, piece, ss7.at[t, f, e], rs7.at[t, f, e], beside).wait_recv()

        for e in range(1, NX):
            first_copy(e).start()
        for e in (0, 1, 3, 2):
            if e:
                piece = block(core, e, 0)
                copy(piece, piece, ss5.at[t, e], rs5.at[t, e], beside).wait_recv()
            second_copy(e, 1).start()
            second_copy(e, 3).start()
            to_core(e, 0).start()

        def relay(e):
            for f in (1, 3):
                second_wait(e, f)
                relay_copy(e, f).start()
                to_core(e, f).start()

        def last(e):
            relay_wait(e, 1)
            relay_wait(e, 3)
            to_core(e, 2).start()

        events = {1: [(relay, 0)], 3: [(relay, 1)], 5: [(relay, 3)], 6: [(relay, 2)],
                  9: [(last, 0)], 11: [(last, 1)], 13: [(last, 3)], 15: [(last, 2)]}

        def nth(k):
            e = sum(jnp.where(k == n, v[0], 0) for n, v in enumerate(ORDER) if v[0])
            f = sum(jnp.where(k == n, v[1], 0) for n, v in enumerate(ORDER) if v[1])
            return e, f

        keep = lax.rem(lanes((ROWS_LOC, 256)), 128) < BW

        @pl.loop(0, CHUNKS)
        def _(k):
            for n, steps in events.items():
                @pl.when(k == n)
                def _():
                    for step, e in steps:
                        step(e)

            e, f = nth(k)
            core_wait(e, f)
            chunk = where(e, f)
            slots = slots_of(chunk)
            before = None
            for j in range(PER):
                at = pl.ds(pl.multiple_of(chunk * WIDE + 256 * j, 256), 256)
                now = rotate_group(
                    slots[j], src[:, at],
                    [rot[t, c, chunk, j, 0] for c in range(2)],
                    [rot[t, c, chunk, j, 1] for c in range(2)],
                )
                odd = dst[:, at] if before is None else before
                dst[:, at] = jnp.where(keep, now, odd)
                before = now
            at = columns(ahead(chunk, 1, CHUNKS), 0, 256)
            dst[:, at] = jnp.where(keep, dst[:, at], before)

        @pl.loop(0, CHUNKS)
        def _(s):
            core_copy(s).wait_send()

        @pl.loop(0, CHUNKS - 1)
        def _(s):
            plane_copy(s).wait_send()

        for e in range(1, NX):
            first_copy(e).wait_send()

        @pl.loop(0, NX)
        def _(e):
            for f in (1, 3):
                second_copy(e, f).wait_send()
                relay_copy(e, f).wait_send()
            for f in range(NX):
                to_core(e, f).wait_send()

    for t in range(STEPS):
        turn(t)


def local(matrix, pairing):
    dma = pltpu.SemaphoreType.DMA
    shapes = [(CHUNKS,), (CHUNKS,), (NZ,), (NZ,), (NX,), (NX, 5), (NX, NX)]
    vmem = pltpu.VMEM
    return pl.pallas_call(
        body,
        out_shape=pltpu.VMEM(matrix.shape, matrix.dtype),
        in_specs=[pl.BlockSpec(memory_space=pltpu.VMEM), pl.BlockSpec(memory_space=pl.ANY)],
        out_specs=pl.BlockSpec(memory_space=pltpu.VMEM),
        scratch_shapes=[
            vmem((2, ROWS_LOC, 256 * GROUPS), jnp.bfloat16),
            vmem((PER, 256, 256), jnp.float32),
            vmem((STEPS, CHUNKS, 2, PAY, 128), jnp.bfloat16),
            vmem((STEPS, CHUNKS, PAY, 128), jnp.bfloat16),
            vmem((STEPS, CHUNKS - 1, PAY, 128), jnp.bfloat16),
            vmem((STEPS, CHUNKS - 1, PAY, 128), jnp.bfloat16),
            vmem((STEPS, PER, 40, 128), jnp.float32),
            vmem((STEPS, NZ, 40, 128), jnp.float32),
            vmem((STEPS, 2, CHUNKS, PER, 2, BW, 128), jnp.bfloat16),
        ]
        + [dma((CHUNKS,))]
        + [dma((STEPS,) + shape) for shape in shapes for _ in range(2)],
        compiler_params=pltpu.CompilerParams(
            collective_id=0, has_side_effects=True, vmem_limit_bytes=48 * 2**20
        ),
    )(pairing.reshape(STEPS * CHUNKS, 4 * PER), matrix)


def solution(mesh):
    placed = (P(("row", "blk"), None), P())
    return jax.shard_map(
        local, mesh=mesh, in_specs=placed, out_specs=P(("row", "blk"), None), check_vma=False
    )
```

```python
import jax
import jax.numpy as jnp
from jax import lax
from jax.experimental import pallas as pl
from jax.experimental.pallas import tpu as pltpu
from jax.sharding import PartitionSpec as P

BW = 64
STEPS = 2
XH, XL, NY, NZ = 2, 2, 4, 8
NX = XH * XL
CHUNKS = NX * NY
PER = NZ // 2
GROUPS = CHUNKS * PER
ROWS_LOC = 192
CROSS_ROWS = 32 * PER
PAY = CROSS_ROWS + 16
WIDE = 256 * PER
HIGH = lax.Precision.HIGHEST
MESH = pl.DeviceIdType.MESH
ORDER = [(0, 0), (0, 1), (0, 3), (1, 0), (3, 0), (1, 1), (1, 3), (3, 1), (3, 3),
         (0, 2), (2, 0), (1, 2), (2, 1), (3, 2), (2, 3), (2, 2)]


def lanes(shape):
    return lax.broadcasted_iota(jnp.int32, shape, len(shape) - 1)


def gram_of(xg):
    return lax.dot_general(
        xg, xg, (((0,), (0,)), ((), ())), preferred_element_type=jnp.float32
    )


def group_payload(slots, j, gscr):
    row = lax.broadcasted_iota(jnp.int32, (BW, 128), 0)
    lane = lanes((BW, 128))
    sq = []
    for t in range(2):
        tile = slice(128 * t, 128 * t + 128)
        first = jnp.where(lane == row, gscr[j, 128 * t : 128 * t + BW, tile], 0.0)
        second = jnp.where(lane == row + BW, gscr[j, 128 * t + BW : 128 * t + 128, tile], 0.0)
        sq.append(jnp.sum(first + second, axis=0, keepdims=True))
    turned_sq = [pltpu.roll(v, BW, 1) for v in sq]
    lane32 = lanes((32, 128)) < BW
    lane1 = lanes((1, 128)) < BW
    cross, squares = [], []
    for c in range(2):
        a, b = slots[2 * c], slots[2 * c + 1]
        high_b = jnp.broadcast_to(b >= 2, (BW, 128))
        tile = None
        for s in range(4):
            rows = slice(BW * s, BW * s + BW)
            part = jnp.where(high_b, gscr[j, rows, 128:], gscr[j, rows, :128])
            tile = part if tile is None else jnp.where(
                jnp.broadcast_to(a == s, (BW, 128)), part, tile
            )
        turned = pltpu.roll(tile, BW, 1)
        odd_b = (b == 1) | (b == 3)
        odd = jnp.broadcast_to(odd_b, (32, 128))
        low = jnp.where(odd, turned[:32], tile[:32])
        high = jnp.where(odd, tile[32:], turned[32:])
        cross.append(jnp.where(lane32, low, high).astype(jnp.bfloat16))
        sa = jnp.where(a == 0, sq[0], jnp.where(
            a == 1, turned_sq[0], jnp.where(a == 2, sq[1], turned_sq[1])))
        sb = jnp.where(b == 0, turned_sq[0], jnp.where(
            b == 1, sq[0], jnp.where(b == 2, turned_sq[1], sq[1])))
        squares.append(jnp.where(lane1, sa, sb))
    return cross, squares


def rotate_group(slots, xg, left, right):
    lane = lanes((BW, 128)) < BW
    zero = jnp.zeros((BW, 128), jnp.bfloat16)
    tiles = []
    for c in range(2):
        a, b = [jnp.broadcast_to(slots[2 * c + k], (BW, 128)) for k in range(2)]
        top = jnp.where(lane, left[c], right[c])
        bot = pltpu.roll(jnp.where(lane, right[c], left[c]), BW, 1)
        tiles.append(jnp.concatenate(
            [jnp.where(a == s, top, jnp.where(b == s, bot, zero)) for s in range(4)], axis=0
        ))
    return jnp.dot(
        xg, jnp.concatenate(tiles, axis=1), preferred_element_type=jnp.float32
    ).astype(jnp.bfloat16)


def half_rotations(packed, squares):
    raw = jnp.concatenate([packed[:, :BW], packed[:, BW:]], axis=0)
    scale = 1.0 / jnp.sqrt(squares + 1e-06)
    row = lax.broadcasted_iota(jnp.int32, (BW, BW), 0)
    col = lax.broadcasted_iota(jnp.int32, (BW, BW), 1)
    eye = row == col
    left_scale = jnp.sum(jnp.where(eye, scale[:, :BW], 0.0), axis=1, keepdims=True)
    cross = 0.5 * raw * left_scale * scale[:, BW:]
    crossed = cross.T
    unit = jnp.where(eye, 1.0, 0.0)
    number = lax.broadcasted_iota(jnp.int32, (BW, 1), 0)
    pairs = [(cross, crossed), (crossed, cross)]
    work = [
        jnp.concatenate(
            [unit + jnp.dot(u, v, precision=HIGH, preferred_element_type=jnp.float32), unit],
            axis=1,
        )
        for u, v in pairs
    ]
    for k in range(0, BW - 2, 2):
        for side in range(2):
            m = work[side]
            p, q, r = [
                jnp.broadcast_to(m[i : i + 1, j : j + 1], (1, 128))
                for i, j in ((k, k), (k, k + 1), (k + 1, k + 1))
            ]
            inverse = 1.0 / (p * r - q * q)
            over, under = m[k : k + 1, :], m[k + 1 : k + 2, :]
            one = (r * over - q * under) * inverse
            two = (p * under - q * over) * inverse
            below = number > k + 1
            work[side] = m - (
                jnp.where(below, m[:, k : k + 1], 0.0) * one
                + jnp.where(below, m[:, k + 1 : k + 2], 0.0) * two
            )
    for side in range(2):
        m = work[side]
        pivot = jnp.sum(jnp.where(eye, m[:, :BW], 0.0), axis=1, keepdims=True)
        beside = jnp.sum(jnp.where(row == col + 1, m[:, :BW], 0.0), axis=1, keepdims=True)
        above = pltpu.roll(jnp.broadcast_to(pivot, (BW, 128)), 1, 0)
        odd = jnp.where(lax.rem(number, 2) == 1, beside, 0.0)
        work[side] = m - odd / above * pltpu.roll(m, 1, 0)
    halves = []
    for side in range(2):
        m = work[side]
        diag = jnp.sum(jnp.where(eye, m[:, :BW], 0.0), axis=1, keepdims=True)
        upper = (m[:, BW:] * lax.rsqrt(diag)).T
        other = jnp.dot(
            pairs[side][1], upper, precision=HIGH, preferred_element_type=jnp.float32
        )
        halves.append(jnp.concatenate([upper, other if side else -other], axis=1))
    return [half.astype(jnp.bfloat16) for half in halves]


def body(pair, matrix, out, cur, gscr, pay, got0, sent1, got1, sent2, got2, rot, *sems):
    (ins, ss0, rs0, ss1, rs1, ss2, rs2, ss4, rs4, ss5, rs5, ss6, rs6, ss7, rs7) = sems
    row, blk = lax.axis_index("row"), lax.axis_index("blk")
    core = lax.rem(row, 2)
    z = lax.rem(blk, NZ)
    x = (row // 2) * XL + lax.rem(blk // NZ, XL)
    y = blk // (NZ * XL)
    sibling = 1 - core
    own = x * NY + y
    mine = z // 2
    owner = lax.rem(z, 2) == core

    def device(x, y, z, core):
        return {"row": (x // XL) * 2 + core, "blk": (y * XL + lax.rem(x, XL)) * NZ + z}

    beside = device(x, y, z, sibling)

    def ahead(v, d, n):
        return lax.rem(v + d, n)

    def behind(v, d, n):
        return lax.rem(v + (n - d), n)

    def plane(d):
        there = ahead(own, d, CHUNKS)
        return device(there // NY, lax.rem(there, NY), z, core)

    def copy(src, dst, send_sem, recv_sem, target):
        return pltpu.make_async_remote_copy(
            src_ref=src, dst_ref=dst, send_sem=send_sem, recv_sem=recv_sem,
            device_id=target, device_id_type=MESH,
        )

    def columns(chunk, first=0, count=WIDE):
        return pl.ds(pl.multiple_of(chunk * WIDE + first, 256), count)

    def load(s):
        at = columns(ahead(own, s + 1, CHUNKS))
        return pltpu.make_async_copy(matrix.at[:, at], cur.at[0, :, at], ins.at[s])

    @pl.loop(0, CHUNKS)
    def _(s):
        load(s).start()

    barrier = pltpu.get_barrier_semaphore()
    greeted = [plane(d) for d in range(1, CHUNKS)] + [beside]
    greeted += [device(x, y, ahead(z, dz, NZ), core) for dz in range(1, NZ)]
    for peer in greeted:
        pl.semaphore_signal(barrier, inc=1, device_id=peer, device_id_type=MESH)

    def turn(t):
        src, dst = cur.at[t], cur.at[1] if t == 0 else out

        def slots_of(chunk):
            table = pair[t].astype(jnp.float32)
            lane = lanes(table.shape)
            slots = []
            for j in range(PER):
                picked = jnp.where(lane == chunk * PER + j, table, 0.0)
                numbers = jnp.sum(picked, axis=1, keepdims=True)
                slots.append([jnp.broadcast_to(numbers[n : n + 1], (1, 128)) for n in range(4)])
            return slots

        def core_copy(s):
            return copy(pay.at[t, s, sibling], got0.at[t, s], ss0.at[t, s], rs0.at[t, s], beside)

        def plane_copy(s):
            return copy(sent1.at[t, s], got1.at[t, s], ss1.at[t, s], rs1.at[t, s], plane(s + 1))

        def summed(s):
            core_copy(s).wait_recv()
            return pay[t, s, core].astype(jnp.float32) + got0[t, s].astype(jnp.float32)

        def pass_on(s):
            sent1[t, s] = summed(s).astype(jnp.bfloat16)
            plane_copy(s).start()

        def gram_chunk(s, u):
            chunk = ahead(own, s + 1, CHUNKS)
            for j in range(PER):
                at = pl.ds(pl.multiple_of(chunk * WIDE + 256 * j, 256), 256)
                gscr[u, j] = gram_of(src[:, at])
            slots = slots_of(chunk)
            row16 = lax.broadcasted_iota(jnp.int32, (16, 128), 0)
            squares = [jnp.zeros((16, 128), jnp.float32)] * 2
            for j in range(PER):
                cross, sq = group_payload(slots[j], j, gscr.at[u])
                for c in range(2):
                    pay[t, s, c, 32 * j : 32 * j + 32] = cross[c]
                    squares[c] = jnp.where(row16 == j, sq[c], squares[c])
            for c in range(2):
                pay[t, s, c, CROSS_ROWS:] = squares[c].astype(jnp.bfloat16)

        @pl.loop(0, CHUNKS // 2)
        def _(k):
            if t == 0:
                for u in range(2):
                    load(2 * k + u).wait()
            for u in range(2):
                gram_chunk(2 * k + u, u)
            if t == 0:
                @pl.when(k == 0)
                def _():
                    pl.semaphore_wait(barrier, len(greeted))

            for u in range(2):
                core_copy(2 * k + u).start()

            @pl.when(k > 0)
            def _():
                for u in range(2):
                    pass_on(2 * k - 2 + u)

        pass_on(CHUNKS - 2)
        total = summed(CHUNKS - 1)
        for s in range(CHUNKS - 1):
            plane_copy(s).wait_recv()
            total = total + got1[t, s].astype(jnp.float32)

        for j in range(PER):
            sent2[t, j, :32] = total[32 * j : 32 * j + 32]
            sent2[t, j, 32:] = total[CROSS_ROWS : CROSS_ROWS + 8]

        def sum_copy(dz):
            there = ahead(z, dz, NZ)
            return copy(sent2.at[t, there // 2], got2.at[t, dz], ss2.at[t, dz], rs2.at[t, dz],
                        device(x, y, there, core))

        def gather_copy(dz, at):
            piece = rot.at[t, core, own, at]
            return copy(piece, piece, ss4.at[t, dz], rs4.at[t, dz],
                        device(x, y, ahead(z, dz, NZ), core))

        @pl.when(owner)
        def _():
            for dz in range(2, NZ, 2):
                sum_copy(dz).start()
            got = sent2[t, mine]
            for dz in range(1, NZ):
                sum_copy(dz).wait_recv()
                got = got + got2[t, dz]
            pick = lax.broadcasted_iota(jnp.int32, (8, 128), 0) == mine
            squares = jnp.sum(jnp.where(pick, got[32:], 0.0), axis=0, keepdims=True)
            halves = half_rotations(got[:32], squares)
            for side in range(2):
                rot[t, core, own, mine, side] = halves[side]
            for dz in range(1, NZ):
                gather_copy(dz, mine).start()
            for dz in range(2, NZ, 2):
                gather_copy(dz, behind(z, dz, NZ) // 2).wait_recv()
            for dz in range(2, NZ, 2):
                sum_copy(dz).wait_send()
            for dz in range(1, NZ):
                gather_copy(dz, mine).wait_send()

        @pl.when(jnp.logical_not(owner))
        def _():
            for dz in range(1, NZ, 2):
                sum_copy(dz).start()
            for dz in range(1, NZ, 2):
                gather_copy(dz, behind(z, dz, NZ) // 2).wait_recv()
            for dz in range(1, NZ, 2):
                sum_copy(dz).wait_send()

        def where(e, f):
            bx = behind(x, core * e + (1 - core) * f, NX)
            by = behind(y, (1 - core) * e + core * f, NY)
            return bx * NY + by

        def block(which, e, f, part=None):
            piece = rot.at[t, which, where(e, f)]
            return piece if part is None else piece.at[pl.ds(part * (PER // 2), PER // 2)]

        def along(e, f):
            return device(
                ahead(x, core * e + (1 - core) * f, NX),
                ahead(y, (1 - core) * e + core * f, NY), z, core,
            )

        def first_copy(e):
            return copy(block(core, 0, 0), block(core, 0, 0), ss5.at[t, e], rs5.at[t, e],
                        along(e, 0))

        def second_copy(e, f):
            piece = block(core, e, 0)
            return copy(piece, piece, ss6.at[t, e, f], rs6.at[t, e, f], along(0, f))

        def second_wait(e, f):
            piece = block(core, e, f)
            copy(piece, piece, ss6.at[t, e, f], rs6.at[t, e, f], beside).wait_recv()

        def relay_copy(e, f):
            piece = block(core, e, f, f // 2)
            k = f - f // 2 * 3
            return copy(piece, piece, ss6.at[t, e, 2 * k], rs6.at[t, e, 2 * k], along(0, f))

        def relay_wait(e, f):
            piece = block(core, e, 2, f // 2)
            k = f - f // 2 * 3
            copy(piece, piece, ss6.at[t, e, 2 * k], rs6.at[t, e, 2 * k], beside).wait_recv()

        def to_core(e, f):
            piece = block(core, e, f)
            return copy(piece, piece, ss7.at[t, e, f], rs7.at[t, e, f], beside)

        def core_wait(e, f):
            piece = block(sibling, e, f)
            copy(piece, piece, ss7.at[t, f, e], rs7.at[t, f, e], beside).wait_recv()

        for e in range(1, NX):
            first_copy(e).start()
        for e in (0, 1, 3, 2):
            if e:
                piece = block(core, e, 0)
                copy(piece, piece, ss5.at[t, e], rs5.at[t, e], beside).wait_recv()
            second_copy(e, 1).start()
            second_copy(e, 3).start()
            to_core(e, 0).start()

        def relay(e):
            for f in (1, 3):
                second_wait(e, f)
                relay_copy(e, f).start()
                to_core(e, f).start()

        def last(e):
            relay_wait(e, 1)
            relay_wait(e, 3)
            to_core(e, 2).start()

        events = {0: [(relay, 0)], 1: [(relay, 1)], 2: [(relay, 3)], 3: [(relay, 2)],
                  4: [(last, 0)], 5: [(last, 1)], 6: [(last, 3)], 7: [(last, 2)]}

        def nth(k):
            e = sum(jnp.where(k == n, v[0], 0) for n, v in enumerate(ORDER) if v[0])
            f = sum(jnp.where(k == n, v[1], 0) for n, v in enumerate(ORDER) if v[1])
            return e, f

        keep = lax.rem(lanes((ROWS_LOC, 256)), 128) < BW

        def rotate_chunk(chunk):
            slots = slots_of(chunk)
            before = None
            for j in range(PER):
                at = pl.ds(pl.multiple_of(chunk * WIDE + 256 * j, 256), 256)
                now = rotate_group(
                    slots[j], src[:, at],
                    [rot[t, c, chunk, j, 0] for c in range(2)],
                    [rot[t, c, chunk, j, 1] for c in range(2)],
                )
                odd = dst[:, at] if before is None else before
                dst[:, at] = jnp.where(keep, now, odd)
                before = now
            at = columns(ahead(chunk, 1, CHUNKS), 0, 256)
            dst[:, at] = jnp.where(keep, dst[:, at], before)

        @pl.loop(0, CHUNKS // 2)
        def _(k):
            for n, steps in events.items():
                @pl.when(k == n)
                def _():
                    for step, e in steps:
                        step(e)

            both = [nth(2 * k + u) for u in range(2)]
            for e, f in both:
                core_wait(e, f)
            for e, f in both:
                rotate_chunk(where(e, f))

        @pl.loop(0, CHUNKS)
        def _(s):
            core_copy(s).wait_send()

        @pl.loop(0, CHUNKS - 1)
        def _(s):
            plane_copy(s).wait_send()

        for e in range(1, NX):
            first_copy(e).wait_send()

        @pl.loop(0, NX)
        def _(e):
            for f in (1, 3):
                second_copy(e, f).wait_send()
                relay_copy(e, f).wait_send()
            for f in range(NX):
                to_core(e, f).wait_send()

    for t in range(STEPS):
        turn(t)


def local(matrix, pairing):
    dma = pltpu.SemaphoreType.DMA
    shapes = [(CHUNKS,), (CHUNKS,), (NZ,), (NZ,), (NX,), (NX, 5), (NX, NX)]
    vmem = pltpu.VMEM
    return pl.pallas_call(
        body,
        out_shape=pltpu.VMEM(matrix.shape, matrix.dtype),
        in_specs=[pl.BlockSpec(memory_space=pltpu.VMEM), pl.BlockSpec(memory_space=pl.ANY)],
        out_specs=pl.BlockSpec(memory_space=pltpu.VMEM),
        scratch_shapes=[
            vmem((2, ROWS_LOC, 256 * GROUPS), jnp.bfloat16),
            vmem((2, PER, 256, 256), jnp.float32),
            vmem((STEPS, CHUNKS, 2, PAY, 128), jnp.bfloat16),
            vmem((STEPS, CHUNKS, PAY, 128), jnp.bfloat16),
            vmem((STEPS, CHUNKS - 1, PAY, 128), jnp.bfloat16),
            vmem((STEPS, CHUNKS - 1, PAY, 128), jnp.bfloat16),
            vmem((STEPS, PER, 40, 128), jnp.float32),
            vmem((STEPS, NZ, 40, 128), jnp.float32),
            vmem((STEPS, 2, CHUNKS, PER, 2, BW, 128), jnp.bfloat16),
        ]
        + [dma((CHUNKS,))]
        + [dma((STEPS,) + shape) for shape in shapes for _ in range(2)],
        compiler_params=pltpu.CompilerParams(
            collective_id=0, has_side_effects=True, vmem_limit_bytes=48 * 2**20
        ),
    )(jnp.transpose(pairing, (0, 2, 1)), matrix)


def solution(mesh):
    placed = (P(("row", "blk"), None), P())
    return jax.shard_map(
        local, mesh=mesh, in_specs=placed, out_specs=P(("row", "blk"), None), check_vma=False
    )
```

```python
import jax
import jax.numpy as jnp
from jax import lax
from jax.experimental import pallas as pl
from jax.experimental.pallas import tpu as pltpu
from jax.sharding import PartitionSpec as P

BW = 64
STEPS = 2
XH, XL, NY, NZ = 2, 2, 4, 8
NX = XH * XL
CHUNKS = NX * NY
PER = NZ // 2
GROUPS = CHUNKS * PER
ROWS_LOC = 192
CROSS_ROWS = 32 * PER
PAY = CROSS_ROWS + 16
WIDE = 256 * PER
HIGH = lax.Precision.HIGHEST
MESH = pl.DeviceIdType.MESH
ORDER = [(0, 0), (0, 1), (0, 3), (1, 0), (3, 0), (1, 1), (1, 3), (3, 1), (3, 3),
         (0, 2), (2, 0), (1, 2), (2, 1), (3, 2), (2, 3), (2, 2)]


def lanes(shape):
    return lax.broadcasted_iota(jnp.int32, shape, len(shape) - 1)


def gram_of(xg):
    return lax.dot_general(
        xg, xg, (((0,), (0,)), ((), ())), preferred_element_type=jnp.float32
    )


def group_payload(slots, j, gscr):
    row = lax.broadcasted_iota(jnp.int32, (BW, 128), 0)
    lane = lanes((BW, 128))
    sq = []
    for t in range(2):
        tile = slice(128 * t, 128 * t + 128)
        first = jnp.where(lane == row, gscr[j, 128 * t : 128 * t + BW, tile], 0.0)
        second = jnp.where(lane == row + BW, gscr[j, 128 * t + BW : 128 * t + 128, tile], 0.0)
        sq.append(jnp.sum(first + second, axis=0, keepdims=True))
    turned_sq = [pltpu.roll(v, BW, 1) for v in sq]
    lane32 = lanes((32, 128)) < BW
    lane1 = lanes((1, 128)) < BW
    cross, squares = [], []
    for c in range(2):
        a, b = slots[2 * c], slots[2 * c + 1]
        high_b = jnp.broadcast_to(b >= 2, (BW, 128))
        tile = None
        for s in range(4):
            rows = slice(BW * s, BW * s + BW)
            part = jnp.where(high_b, gscr[j, rows, 128:], gscr[j, rows, :128])
            tile = part if tile is None else jnp.where(
                jnp.broadcast_to(a == s, (BW, 128)), part, tile
            )
        turned = pltpu.roll(tile, BW, 1)
        odd_b = (b == 1) | (b == 3)
        odd = jnp.broadcast_to(odd_b, (32, 128))
        low = jnp.where(odd, turned[:32], tile[:32])
        high = jnp.where(odd, tile[32:], turned[32:])
        cross.append(jnp.where(lane32, low, high).astype(jnp.bfloat16))
        sa = jnp.where(a == 0, sq[0], jnp.where(
            a == 1, turned_sq[0], jnp.where(a == 2, sq[1], turned_sq[1])))
        sb = jnp.where(b == 0, turned_sq[0], jnp.where(
            b == 1, sq[0], jnp.where(b == 2, turned_sq[1], sq[1])))
        squares.append(jnp.where(lane1, sa, sb))
    return cross, squares


def rotate_group(slots, xg, left, right):
    lane = lanes((BW, 128)) < BW
    zero = jnp.zeros((BW, 128), jnp.bfloat16)
    tiles = []
    for c in range(2):
        a, b = [jnp.broadcast_to(slots[2 * c + k], (BW, 128)) for k in range(2)]
        top = jnp.where(lane, left[c], right[c])
        bot = pltpu.roll(jnp.where(lane, right[c], left[c]), BW, 1)
        tiles.append(jnp.concatenate(
            [jnp.where(a == s, top, jnp.where(b == s, bot, zero)) for s in range(4)], axis=0
        ))
    return jnp.dot(
        xg, jnp.concatenate(tiles, axis=1), preferred_element_type=jnp.float32
    ).astype(jnp.bfloat16)


def half_rotations(packed, squares):
    raw = jnp.concatenate([packed[:, :BW], packed[:, BW:]], axis=0)
    scale = 1.0 / jnp.sqrt(squares + 1e-06)
    row = lax.broadcasted_iota(jnp.int32, (BW, BW), 0)
    col = lax.broadcasted_iota(jnp.int32, (BW, BW), 1)
    eye = row == col
    left_scale = jnp.sum(jnp.where(eye, scale[:, :BW], 0.0), axis=1, keepdims=True)
    cross = 0.5 * raw * left_scale * scale[:, BW:]
    crossed = cross.T
    unit = jnp.where(eye, 1.0, 0.0)
    number = lax.broadcasted_iota(jnp.int32, (BW, 1), 0)
    pairs = [(cross, crossed), (crossed, cross)]
    work = [
        jnp.concatenate(
            [unit + jnp.dot(u, v, precision=HIGH, preferred_element_type=jnp.float32), unit],
            axis=1,
        )
        for u, v in pairs
    ]
    for k in range(0, BW - 2, 2):
        for side in range(2):
            m = work[side]
            p, q, r = [
                jnp.broadcast_to(m[i : i + 1, j : j + 1], (1, 128))
                for i, j in ((k, k), (k, k + 1), (k + 1, k + 1))
            ]
            inverse = 1.0 / (p * r - q * q)
            over, under = m[k : k + 1, :], m[k + 1 : k + 2, :]
            one = (r * over - q * under) * inverse
            two = (p * under - q * over) * inverse
            below = number > k + 1
            work[side] = m - (
                jnp.where(below, m[:, k : k + 1], 0.0) * one
                + jnp.where(below, m[:, k + 1 : k + 2], 0.0) * two
            )
    for side in range(2):
        m = work[side]
        pivot = jnp.sum(jnp.where(eye, m[:, :BW], 0.0), axis=1, keepdims=True)
        beside = jnp.sum(jnp.where(row == col + 1, m[:, :BW], 0.0), axis=1, keepdims=True)
        above = pltpu.roll(jnp.broadcast_to(pivot, (BW, 128)), 1, 0)
        odd = jnp.where(lax.rem(number, 2) == 1, beside, 0.0)
        work[side] = m - odd / above * pltpu.roll(m, 1, 0)
    halves = []
    for side in range(2):
        m = work[side]
        diag = jnp.sum(jnp.where(eye, m[:, :BW], 0.0), axis=1, keepdims=True)
        upper = (m[:, BW:] * lax.rsqrt(diag)).T
        other = jnp.dot(
            pairs[side][1], upper, precision=HIGH, preferred_element_type=jnp.float32
        )
        halves.append(jnp.concatenate([upper, other if side else -other], axis=1))
    return [half.astype(jnp.bfloat16) for half in halves]


def body(pair, matrix, out, cur, gscr, pay, got0, sent1, got1, sent2, got2, rot, *sems):
    (ins, ss0, rs0, ss1, rs1, ss2, rs2, ss4, rs4, ss5, rs5, ss6, rs6, ss7, rs7) = sems
    row, blk = lax.axis_index("row"), lax.axis_index("blk")
    core = lax.rem(row, 2)
    z = lax.rem(blk, NZ)
    x = (row // 2) * XL + lax.rem(blk // NZ, XL)
    y = blk // (NZ * XL)
    sibling = 1 - core
    own = x * NY + y
    mine = z // 2
    owner = lax.rem(z, 2) == core

    def device(x, y, z, core):
        return {"row": (x // XL) * 2 + core, "blk": (y * XL + lax.rem(x, XL)) * NZ + z}

    beside = device(x, y, z, sibling)

    def ahead(v, d, n):
        return lax.rem(v + d, n)

    def behind(v, d, n):
        return lax.rem(v + (n - d), n)

    def plane(d):
        there = ahead(own, d, CHUNKS)
        return device(there // NY, lax.rem(there, NY), z, core)

    def copy(src, dst, send_sem, recv_sem, target):
        return pltpu.make_async_remote_copy(
            src_ref=src, dst_ref=dst, send_sem=send_sem, recv_sem=recv_sem,
            device_id=target, device_id_type=MESH,
        )

    def columns(chunk, first=0, count=WIDE):
        return pl.ds(pl.multiple_of(chunk * WIDE + first, 256), count)

    def load(s):
        at = columns(ahead(own, s + 1, CHUNKS))
        return pltpu.make_async_copy(matrix.at[:, at], cur.at[0, :, at], ins.at[s])

    @pl.loop(0, CHUNKS)
    def _(s):
        load(s).start()

    barrier = pltpu.get_barrier_semaphore()
    greeted = [plane(d) for d in range(1, CHUNKS)] + [beside]
    greeted += [device(x, y, ahead(z, dz, NZ), core) for dz in range(1, NZ)]
    for peer in greeted:
        pl.semaphore_signal(barrier, inc=1, device_id=peer, device_id_type=MESH)

    def turn(t):
        src, dst = cur.at[t], cur.at[1] if t == 0 else out

        def slots_of(chunk):
            table = pair[t].astype(jnp.float32)
            lane = lanes(table.shape)
            slots = []
            for j in range(PER):
                picked = jnp.where(lane == chunk * PER + j, table, 0.0)
                numbers = jnp.sum(picked, axis=1, keepdims=True)
                slots.append([jnp.broadcast_to(numbers[n : n + 1], (1, 128)) for n in range(4)])
            return slots

        def core_copy(s):
            return copy(pay.at[t, s, sibling], got0.at[t, s], ss0.at[t, s], rs0.at[t, s], beside)

        def plane_copy(s):
            return copy(sent1.at[t, s], got1.at[t, s], ss1.at[t, s], rs1.at[t, s], plane(s + 1))

        def summed(s):
            core_copy(s).wait_recv()
            return pay[t, s, core].astype(jnp.float32) + got0[t, s].astype(jnp.float32)

        def pass_on(s):
            sent1[t, s] = summed(s).astype(jnp.bfloat16)
            plane_copy(s).start()

        def gram_chunk(s, u):
            chunk = ahead(own, s + 1, CHUNKS)
            for j in range(PER):
                at = pl.ds(pl.multiple_of(chunk * WIDE + 256 * j, 256), 256)
                gscr[u, j] = gram_of(src[:, at])
            slots = slots_of(chunk)
            row16 = lax.broadcasted_iota(jnp.int32, (16, 128), 0)
            squares = [jnp.zeros((16, 128), jnp.float32)] * 2
            for j in range(PER):
                cross, sq = group_payload(slots[j], j, gscr.at[u])
                for c in range(2):
                    pay[t, s, c, 32 * j : 32 * j + 32] = cross[c]
                    squares[c] = jnp.where(row16 == j, sq[c], squares[c])
            for c in range(2):
                pay[t, s, c, CROSS_ROWS:] = squares[c].astype(jnp.bfloat16)

        @pl.loop(0, CHUNKS // 2)
        def _(k):
            if t == 0:
                for u in range(2):
                    load(2 * k + u).wait()
            for u in range(2):
                gram_chunk(2 * k + u, u)
            if t == 0:
                @pl.when(k == 0)
                def _():
                    pl.semaphore_wait(barrier, len(greeted))

            for u in range(2):
                core_copy(2 * k + u).start()

            @pl.when(k > 0)
            def _():
                for u in range(2):
                    pass_on(2 * k - 2 + u)

        pass_on(CHUNKS - 2)
        total = summed(CHUNKS - 1)
        for s in range(CHUNKS - 1):
            plane_copy(s).wait_recv()
            total = total + got1[t, s].astype(jnp.float32)

        for j in range(PER):
            sent2[t, j, :32] = total[32 * j : 32 * j + 32]
            sent2[t, j, 32:] = total[CROSS_ROWS : CROSS_ROWS + 8]

        def sum_copy(dz):
            there = ahead(z, dz, NZ)
            return copy(sent2.at[t, there // 2], got2.at[t, dz], ss2.at[t, dz], rs2.at[t, dz],
                        device(x, y, there, core))

        def gather_copy(dz, at):
            piece = rot.at[t, core, own, at]
            return copy(piece, piece, ss4.at[t, dz], rs4.at[t, dz],
                        device(x, y, ahead(z, dz, NZ), core))

        def where(e, f):
            bx = behind(x, core * e + (1 - core) * f, NX)
            by = behind(y, (1 - core) * e + core * f, NY)
            return bx * NY + by

        def block(which, e, f, part=None):
            piece = rot.at[t, which, where(e, f)]
            return piece if part is None else piece.at[pl.ds(part * (PER // 2), PER // 2)]

        def along(e, f):
            return device(
                ahead(x, core * e + (1 - core) * f, NX),
                ahead(y, (1 - core) * e + core * f, NY), z, core,
            )

        def first_copy(e, j):
            piece = rot.at[t, core, own, j]
            return copy(piece, piece, ss5.at[t, e, j], rs5.at[t, e, j], along(e, 0))

        def first_wait(e, j):
            piece = rot.at[t, core, where(e, 0), j]
            copy(piece, piece, ss5.at[t, e, j], rs5.at[t, e, j], beside).wait_recv()

        def spread(j):
            for e in range(1, NX):
                first_copy(e, j).start()

        @pl.when(owner)
        def _():
            for dz in range(2, NZ, 2):
                sum_copy(dz).start()
            got = sent2[t, mine]
            for dz in range(1, NZ):
                sum_copy(dz).wait_recv()
                got = got + got2[t, dz]
            pick = lax.broadcasted_iota(jnp.int32, (8, 128), 0) == mine
            squares = jnp.sum(jnp.where(pick, got[32:], 0.0), axis=0, keepdims=True)
            halves = half_rotations(got[:32], squares)
            for side in range(2):
                rot[t, core, own, mine, side] = halves[side]
            for dz in range(1, NZ):
                gather_copy(dz, mine).start()
            spread(mine)
            for dz in (2, 6, 4):
                gather_copy(dz, behind(z, dz, NZ) // 2).wait_recv()
                spread(behind(z, dz, NZ) // 2)
            for dz in range(2, NZ, 2):
                sum_copy(dz).wait_send()
            for dz in range(1, NZ):
                gather_copy(dz, mine).wait_send()

        @pl.when(jnp.logical_not(owner))
        def _():
            for dz in range(1, NZ, 2):
                sum_copy(dz).start()
            for dz in (1, 7, 3, 5):
                gather_copy(dz, behind(z, dz, NZ) // 2).wait_recv()
                spread(behind(z, dz, NZ) // 2)
            for dz in range(1, NZ, 2):
                sum_copy(dz).wait_send()

        def second_copy(e, f):
            piece = block(core, e, 0)
            return copy(piece, piece, ss6.at[t, e, f], rs6.at[t, e, f], along(0, f))

        def second_wait(e, f):
            piece = block(core, e, f)
            copy(piece, piece, ss6.at[t, e, f], rs6.at[t, e, f], beside).wait_recv()

        def relay_copy(e, f):
            piece = block(core, e, f, f // 2)
            k = f - f // 2 * 3
            return copy(piece, piece, ss6.at[t, e, 2 * k], rs6.at[t, e, 2 * k], along(0, f))

        def relay_wait(e, f):
            piece = block(core, e, 2, f // 2)
            k = f - f // 2 * 3
            copy(piece, piece, ss6.at[t, e, 2 * k], rs6.at[t, e, 2 * k], beside).wait_recv()

        def to_core(e, f):
            piece = block(core, e, f)
            return copy(piece, piece, ss7.at[t, e, f], rs7.at[t, e, f], beside)

        def core_wait(e, f):
            piece = block(sibling, e, f)
            copy(piece, piece, ss7.at[t, f, e], rs7.at[t, f, e], beside).wait_recv()

        for e in (0, 1, 3, 2):
            if e:
                for j in range(PER):
                    first_wait(e, j)
            second_copy(e, 1).start()
            second_copy(e, 3).start()
            to_core(e, 0).start()

        def relay(e):
            for f in (1, 3):
                second_wait(e, f)
                relay_copy(e, f).start()
                to_core(e, f).start()

        def last(e):
            relay_wait(e, 1)
            relay_wait(e, 3)
            to_core(e, 2).start()

        events = {0: [(relay, 0)], 1: [(relay, 1)], 2: [(relay, 3)], 3: [(relay, 2)],
                  4: [(last, 0)], 5: [(last, 1)], 6: [(last, 3)], 7: [(last, 2)]}

        def nth(k):
            e = sum(jnp.where(k == n, v[0], 0) for n, v in enumerate(ORDER) if v[0])
            f = sum(jnp.where(k == n, v[1], 0) for n, v in enumerate(ORDER) if v[1])
            return e, f

        keep = lax.rem(lanes((ROWS_LOC, 256)), 128) < BW

        def rotate_chunk(chunk):
            slots = slots_of(chunk)
            before = None
            for j in range(PER):
                at = pl.ds(pl.multiple_of(chunk * WIDE + 256 * j, 256), 256)
                now = rotate_group(
                    slots[j], src[:, at],
                    [rot[t, c, chunk, j, 0] for c in range(2)],
                    [rot[t, c, chunk, j, 1] for c in range(2)],
                )
                odd = dst[:, at] if before is None else before
                dst[:, at] = jnp.where(keep, now, odd)
                before = now
            at = columns(ahead(chunk, 1, CHUNKS), 0, 256)
            dst[:, at] = jnp.where(keep, dst[:, at], before)

        @pl.loop(0, CHUNKS // 2)
        def _(k):
            for n, steps in events.items():
                @pl.when(k == n)
                def _():
                    for step, e in steps:
                        step(e)

            both = [nth(2 * k + u) for u in range(2)]
            for e, f in both:
                core_wait(e, f)
            for e, f in both:
                rotate_chunk(where(e, f))

        @pl.loop(0, CHUNKS)
        def _(s):
            core_copy(s).wait_send()

        @pl.loop(0, CHUNKS - 1)
        def _(s):
            plane_copy(s).wait_send()

        for e in range(1, NX):
            for j in range(PER):
                first_copy(e, j).wait_send()

        @pl.loop(0, NX)
        def _(e):
            for f in (1, 3):
                second_copy(e, f).wait_send()
                relay_copy(e, f).wait_send()
            for f in range(NX):
                to_core(e, f).wait_send()

    for t in range(STEPS):
        turn(t)


def local(matrix, pairing):
    dma = pltpu.SemaphoreType.DMA
    shapes = [(CHUNKS,), (CHUNKS,), (NZ,), (NZ,), (NX, PER), (NX, 5), (NX, NX)]
    vmem = pltpu.VMEM
    return pl.pallas_call(
        body,
        out_shape=pltpu.VMEM(matrix.shape, matrix.dtype),
        in_specs=[pl.BlockSpec(memory_space=pltpu.VMEM), pl.BlockSpec(memory_space=pl.ANY)],
        out_specs=pl.BlockSpec(memory_space=pltpu.VMEM),
        scratch_shapes=[
            vmem((2, ROWS_LOC, 256 * GROUPS), jnp.bfloat16),
            vmem((2, PER, 256, 256), jnp.float32),
            vmem((STEPS, CHUNKS, 2, PAY, 128), jnp.bfloat16),
            vmem((STEPS, CHUNKS, PAY, 128), jnp.bfloat16),
            vmem((STEPS, CHUNKS - 1, PAY, 128), jnp.bfloat16),
            vmem((STEPS, CHUNKS - 1, PAY, 128), jnp.bfloat16),
            vmem((STEPS, PER, 40, 128), jnp.float32),
            vmem((STEPS, NZ, 40, 128), jnp.float32),
            vmem((STEPS, 2, CHUNKS, PER, 2, BW, 128), jnp.bfloat16),
        ]
        + [dma((CHUNKS,))]
        + [dma((STEPS,) + shape) for shape in shapes for _ in range(2)],
        compiler_params=pltpu.CompilerParams(
            collective_id=0, has_side_effects=True, vmem_limit_bytes=48 * 2**20
        ),
    )(jnp.transpose(pairing, (0, 2, 1)), matrix)


def solution(mesh):
    placed = (P(("row", "blk"), None), P())
    return jax.shard_map(
        local, mesh=mesh, in_specs=placed, out_specs=P(("row", "blk"), None), check_vma=False
    )
```
